32 devices in a mesh: ens: 1, tile: 32 (over z, y, x, core).
Axes of the slice: x: 2, y: 2, z: 4, core: 2. Of those that a mesh axis runs over, the one named last changes fastest.
Arguments:
- ocean_field: bfloat16 [131072, 128], P(('ens', 'tile')), may hold values from -6 to 6
- ocean_mask: int32 [131072], P('tile'), may hold values 0 or 1
- remap_weight: bfloat16 [8192, 128, 128], P('tile'), may hold values from -0.125 to 0.125
- source_tile: int32 [8192], P('tile'), may hold values from 0 to 31
- target_tile: int32 [8192], replicated, may hold values from 0 to 15
- dest_device: int32 [8192, 1], replicated, may hold values from 0 to 31, as said below
- atm_state: bfloat16 [65536, 128], P(('ens', 'tile')), may hold values from -6 to 6
- kappa: float32 [65536, 128], P('tile'), may hold values from 0.05 to 0.24
- mix: bfloat16 [128, 128], replicated, may hold values from -0.5 to 0.5
- cotangent: bfloat16 [65536, 128], P(('ens', 'tile')), may hold values from -6 to 6
Outputs:
- atm_next: bfloat16 [65536, 128], P(('ens', 'tile'))
- atm_grad: bfloat16 [65536, 128], P(('ens', 'tile'))
- ocean_grad: bfloat16 [131072, 128], P(('ens', 'tile'))
The draws below stay inside these ranges and needn't reach their ends.
Inputs may be any that keep to these rules, and one draw needn't show every extreme that they name: `dest_device`: the 256 entries of owner device o name only devices o - 4 to o + 4, counted modulo the devices of tile; at most 64 of them name the same device, and in every owner exactly 64 name one device.
All inputs are finite; a program needn't handle non-finite values. No bound on the sum of `ocean_mask` on one device may be relied on, other than what follows from the above.
Results may differ from the reference program's by a relative error of at most 0.0053.
Values may be sent and summed in bfloat16 or wider, within the bound.
A program may use at most 192 MiB of HBM per device.

```python
import math
import jax
import jax.numpy as jnp
from jax import lax

TILE = 128
WIN = 4
AT_DEV = 16
OT_DEV = 32
E_DEV = 256
CAP = 64
CH = 128
ENTRIES = 8192
ATILES = 512
ACELLS = 65536
OCELLS = 131072
N_TILE = 32


def draw_dest_device(key, part):
    key = jax.random.fold_in(key, 11)
    key_main, key_rest = jax.random.split(key)
    heavy = jax.random.randint(key_main, (N_TILE,), 0, 2 * WIN + 1).astype(jnp.int32)

    def per_owner(okey, chosen):
        key_pool, key_order = jax.random.split(okey)
        pool = (jnp.arange(2 * WIN * CAP, dtype=jnp.int32) // CAP).astype(jnp.int32)
        rest = jax.random.permutation(key_pool, pool)[:E_DEV - CAP]
        rest = jnp.where(rest >= chosen, rest + 1, rest)
        offsets = jnp.concatenate([jnp.full((CAP,), chosen, jnp.int32), rest.astype(jnp.int32)])
        return jax.random.permutation(key_order, offsets)
    offsets = jax.vmap(per_owner)(jax.random.split(key_rest, N_TILE), heavy)
    owners = jnp.arange(N_TILE, dtype=jnp.int32)[:, None]
    dest = (owners + offsets - WIN) % N_TILE
    return dest.reshape(ENTRIES, 1).astype(jnp.int32)


def plant(drawn, key, least, high):
    longest = drawn.shape.index(max(drawn.shape))
    spots = []
    for shift in (0, 1):
        where = [jax.random.randint(jax.random.fold_in(key, axis), (), 0, length) for axis, length in enumerate(drawn.shape)]
        where[longest] = (where[longest] + shift) % drawn.shape[longest]
        spots.append(tuple(where))
    return drawn.at[spots[0]].set(least).at[spots[1]].set(high)


def block_levels(stream_key, extent, shards, low, top_value):
    level = 1.0
    for position, blocks in shards:
        steps = jax.random.uniform(jax.random.fold_in(jax.random.fold_in(stream_key, 6), position), (blocks,), jnp.float32, low / len(shards), top_value / len(shards))
        level = level * jnp.repeat(jnp.exp(steps), extent[position] // blocks).reshape((-1,) + (1,) * (len(extent) - 1 - position))
    return level


def bell_draw(key, dims, spread, most, shards=(), held_as=jnp.bfloat16):
    array = jax.random.normal(key, dims, jnp.float32) * spread
    if len(shards) > 0:
        array = block_levels(key, dims, shards, -0.22, 0.18) * array
    return jnp.clip(array, min=-most, max=most).astype(held_as)


def setup_inputs(seed: int = 0, part: int = 0) -> dict:
    arg_keys = jax.random.split(jax.random.key(seed), 11)
    part_keys = jax.random.split(jax.random.fold_in(arg_keys[10], part), 11)
    return {
        "ocean_field": bell_draw(part_keys[0], (OCELLS, CH), 1.0, 6.0, ((0, 32),)),
        "ocean_mask": plant((jax.random.randint(arg_keys[1], (OCELLS,), 0, 4) < 3).astype(jnp.int32), jax.random.fold_in(arg_keys[1], 1), 0, 1),
        "remap_weight": bell_draw(arg_keys[2], (ENTRIES, TILE, TILE), (TILE * E_DEV // AT_DEV) ** -0.5, 0.125, ((0, 32),)),
        "source_tile": plant(jax.random.randint(arg_keys[3], (ENTRIES,), 0, OT_DEV), jax.random.fold_in(arg_keys[3], 1), 0, OT_DEV - 1).astype(jnp.int32),
        "target_tile": plant(jax.random.randint(arg_keys[4], (ENTRIES,), 0, AT_DEV), jax.random.fold_in(arg_keys[4], 1), 0, AT_DEV - 1).astype(jnp.int32),
        "dest_device": draw_dest_device(jax.random.fold_in(arg_keys[10], 71), part),
        "atm_state": bell_draw(part_keys[6], (ACELLS, CH), 1.0, 6.0, ((0, 32),)),
        "kappa": jnp.clip(jnp.exp(math.log(0.24) - 1.5686159 * jax.random.uniform(arg_keys[7], (ACELLS, CH), jnp.float32) ** block_levels(arg_keys[7], (ACELLS, CH), ((0, 32),), -0.2, 0.2)), 0.05, 0.24),
        "mix": bell_draw(arg_keys[8], (CH, CH), CH ** -0.5, 0.5),
        "cotangent": bell_draw(part_keys[9], (ACELLS, CH), 1.0, 6.0, ((0, 32),)),
    }


def laplace(values):
    return jnp.roll(values, 1, axis=0) + jnp.roll(values, -1, axis=0) - 2.0 * values


def reference(ocean_field, ocean_mask, remap_weight, source_tile, target_tile, dest_device, atm_state, kappa, mix, cotangent):
    channels = ocean_field.shape[1]
    keep = (ocean_mask == 1)[:, None]
    masked = jnp.where(keep, ocean_field, jnp.zeros_like(ocean_field))
    ocean_tiles = masked.reshape(OT_DEV * N_TILE, TILE, channels)
    owners = (jnp.arange(ENTRIES, dtype=jnp.int32) // E_DEV).astype(jnp.int32)
    src_global = (owners * OT_DEV + source_tile).astype(jnp.int32)
    tgt_global = (dest_device[:, 0] * AT_DEV + target_tile).astype(jnp.int32)
    weight_blocks = remap_weight.reshape(N_TILE, E_DEV, TILE, TILE)
    src_blocks = src_global.reshape(N_TILE, E_DEV)
    tgt_blocks = tgt_global.reshape(N_TILE, E_DEV)

    def forward_block(total, block):
        weights_blk, sources, targets = block
        picked = ocean_tiles[sources].astype(jnp.float32)
        products = jnp.einsum('eij,ejc->eic', weights_blk.astype(jnp.float32), picked).astype(jnp.bfloat16)
        return total.at[targets].add(products.astype(jnp.float32)), None

    start = jnp.zeros((ATILES, TILE, channels), jnp.float32)
    imported, _ = lax.scan(forward_block, start, (weight_blocks, src_blocks, tgt_blocks))
    forcing = atm_state.astype(jnp.float32) + imported.reshape(ACELLS, channels)
    smooth = forcing + kappa * laplace(forcing)
    tanh_smooth = jnp.tanh(smooth)
    hval = tanh_smooth.astype(jnp.bfloat16)
    atm_next = jnp.dot(hval, mix, preferred_element_type=jnp.float32).astype(jnp.bfloat16)
    grad_tanh = jnp.dot(cotangent, mix.T, preferred_element_type=jnp.float32)
    grad_smooth = grad_tanh * (1.0 - tanh_smooth * tanh_smooth)
    atm_grad = (grad_smooth + laplace(kappa * grad_smooth)).astype(jnp.bfloat16)
    grad_tiles = atm_grad.reshape(ATILES, TILE, channels)

    def adjoint_block(total, block):
        weights_blk, sources, targets = block
        picked = grad_tiles[targets].astype(jnp.float32)
        contrib = jnp.einsum('eji,ejc->eic', weights_blk.astype(jnp.float32), picked)
        return total.at[sources].add(contrib), None

    start_ocean = jnp.zeros((OT_DEV * N_TILE, TILE, channels), jnp.float32)
    ocean_sum, _ = lax.scan(adjoint_block, start_ocean, (weight_blocks, src_blocks, tgt_blocks))
    ocean_sum = ocean_sum.reshape(OCELLS, channels)
    ocean_grad = jnp.where(keep, ocean_sum, jnp.zeros_like(ocean_sum)).astype(jnp.bfloat16)
    return atm_next, atm_grad, ocean_grad
```

```python
import functools

import jax
import jax.numpy as jnp
from jax import lax
from jax.experimental import pallas as pl
from jax.experimental.pallas import tpu as pltpu
from jax.sharding import PartitionSpec as P

WIN = 4
SPAN = 2 * WIN + 1
HALO = 8
STEPS = 16
VMEM_BYTES = 56 * 1024 * 1024
OFFSETS = [o for d in range(1, WIN + 1) for o in (d, -d)]
FAR_FIRST = OFFSETS[::-1]


def diagonal(row, size):
    eye = lax.broadcasted_iota(jnp.int32, (size, size), 0) == lax.broadcasted_iota(
        jnp.int32, (size, size), 1
    )
    return jnp.where(eye, jnp.broadcast_to(row, (size, size)), 0).astype(jnp.bfloat16)


def forward_kernel(per, src_ref, slot_ref, ocean_ref, mask_ref, w_ref, out_ref, acc, xm):
    step = pl.program_id(0)
    tile = w_ref.shape[1]

    @pl.when(step == 0)
    def _():
        def clear(i, carry):
            acc[i] = jnp.zeros(acc.shape[1:], acc.dtype)
            return carry

        lax.fori_loop(0, acc.shape[0], clear, 0)

        def mask_tile(i, carry):
            keep = jnp.where(mask_ref[pl.ds(i, 1), :] == 1, 1.0, 0.0)
            xm[i] = jnp.dot(
                diagonal(keep, tile), ocean_ref[i], preferred_element_type=jnp.float32
            ).astype(jnp.bfloat16)
            return carry

        lax.fori_loop(0, xm.shape[0], mask_tile, 0, unroll=4)

    for k in range(per):
        e = step * per + k
        product = jnp.dot(w_ref[k], xm[src_ref[e]], preferred_element_type=jnp.float32)
        acc[slot_ref[e]] += product

    @pl.when(step == pl.num_programs(0) - 1)
    def _():
        def narrow(i, carry):
            out_ref[i] = acc[i].astype(out_ref.dtype)
            return carry

        lax.fori_loop(0, acc.shape[0], narrow, 0, unroll=4)


def middle_kernel(
    devices, tile, part, atm_ref, kappa_ref, mix_ref, cot_ref,
    near, grad_ref, hval_ref,
    recv, fpad, wpad, gs, gt, lo, hi, lo2, hi2, own,
    psend, precv, hsend, hrecv, gsend, grecv, local_sem,
):
    me = lax.axis_index("tile")
    rows = atm_ref.shape[0]
    tiles = rows // tile

    def at(offset):
        return {"tile": lax.rem(me + offset + devices, devices)}

    def copy_to(src, dst, ssem, rsem, offset):
        return pltpu.make_async_remote_copy(
            src_ref=src, dst_ref=dst, send_sem=ssem, recv_sem=rsem,
            device_id=at(offset), device_id_type=pl.DeviceIdType.MESH,
        )

    barrier = pltpu.get_barrier_semaphore()
    for o in OFFSETS:
        pl.semaphore_signal(
            barrier, inc=1, device_id=at(o), device_id_type=pl.DeviceIdType.MESH
        )
    pl.semaphore_wait(barrier, len(OFFSETS))

    parts = {
        o: copy_to(part.at[o + WIN], recv.at[o + WIN], psend.at[o + WIN], precv.at[o + WIN], o)
        for o in OFFSETS
    }
    for o in FAR_FIRST:
        parts[o].start()
    mine = pltpu.make_async_copy(part.at[WIN], recv.at[WIN], local_sem.at[0])
    mine.start()

    def adjoint_mix(i, carry):
        at_rows = pl.ds(pl.multiple_of(i * tile, tile), tile)
        gt[at_rows, :] = lax.dot_general(
            cot_ref[at_rows, :], mix_ref[...], (((1,), (1,)), ((), ())),
            preferred_element_type=jnp.float32,
        )
        return carry

    lax.fori_loop(0, tiles, adjoint_mix, 0, unroll=2)
    mine.wait()

    def add_parts(slots, first):
        def body(i, carry):
            at_rows = pl.ds(pl.multiple_of(i * tile, tile), tile)
            pad_rows = pl.ds(pl.multiple_of(i * tile + HALO, HALO), tile)
            if first:
                total = atm_ref[at_rows, :].astype(jnp.float32)
            else:
                total = fpad[pad_rows, :]
            for slot in slots:
                total = total + recv[slot, at_rows, :].astype(jnp.float32)
            fpad[pad_rows, :] = total
            return carry

        lax.fori_loop(0, tiles, body, 0)

    add_parts([WIN], True)
    for d in range(1, WIN + 1):
        parts[d].wait_recv()
        parts[-d].wait_recv()
        add_parts([WIN + d, WIN - d], False)

    def edges(pad, low, high, k):
        up = copy_to(pad.at[pl.ds(rows, HALO), :], low, hsend.at[k], hrecv.at[k], 1)
        down = copy_to(pad.at[pl.ds(HALO, HALO), :], high, hsend.at[k + 1], hrecv.at[k + 1], -1)
        return up, down

    def window(pad, i):
        w = pad[pl.ds(pl.multiple_of(i * tile, tile), tile + 2 * HALO), :]
        return w[HALO - 1 : HALO - 1 + tile], w[HALO : HALO + tile], w[HALO + 1 : HALO + 1 + tile]

    fwd_edges = edges(fpad, lo, hi, 0)
    for c in fwd_edges:
        c.start()

    def primal(i, carry):
        at_rows = pl.ds(pl.multiple_of(i * tile, tile), tile)
        before, x, after = window(fpad, i)
        kappa = kappa_ref[at_rows, :]
        th = jnp.tanh(x + kappa * (before + after - 2.0 * x))
        hval_ref[at_rows, :] = th.astype(jnp.bfloat16)
        g = gt[at_rows, :] * (1.0 - th * th)
        gs[at_rows, :] = g
        wpad[pl.ds(pl.multiple_of(i * tile + HALO, HALO), tile), :] = kappa * g
        return carry

    lax.fori_loop(1, tiles - 1, primal, 0)
    for c in fwd_edges:
        c.wait()
    fpad[0:HALO, :] = lo[...]
    fpad[rows + HALO : rows + 2 * HALO, :] = hi[...]
    lax.fori_loop(0, 2, lambda j, c: primal(j * (tiles - 1), c), 0)

    adj_edges = edges(wpad, lo2, hi2, 2)
    for c in adj_edges:
        c.start()

    def adjoint(i, carry):
        at_rows = pl.ds(pl.multiple_of(i * tile, tile), tile)
        before, x, after = window(wpad, i)
        grad = gs[at_rows, :] + before + after - 2.0 * x
        grad_ref[at_rows, :] = grad.astype(jnp.bfloat16)
        own[at_rows, :] = grad.T.astype(jnp.bfloat16)
        return carry

    lax.fori_loop(1, tiles - 1, adjoint, 0)
    pieces = [(tile, rows - 2 * tile), (0, tile), (rows - tile, tile)]

    def grads(p, o):
        cut = pl.ds(pieces[p][0], pieces[p][1])
        slot = WIN - o
        return copy_to(
            own.at[cut, :], near.at[slot, cut, :], gsend.at[p, slot], grecv.at[p, slot], o
        )

    sends = [grads(0, o) for o in FAR_FIRST]
    for c in sends:
        c.start()
    for c in adj_edges:
        c.wait()
    wpad[0:HALO, :] = lo2[...]
    wpad[rows + HALO : rows + 2 * HALO, :] = hi2[...]
    lax.fori_loop(0, 2, lambda j, c: adjoint(j * (tiles - 1), c), 0)
    late = [grads(p, o) for p in (1, 2) for o in FAR_FIRST]
    for c in late:
        c.start()
    keep = pltpu.make_async_copy(own, near.at[WIN], local_sem.at[1])
    keep.start()
    keep.wait()
    for c in sends + late:
        c.wait()
    for o in OFFSETS:
        parts[o].wait_send()


def adjoint_kernel(
    per, src_ref, slot_ref, near_ref, mask_ref, mix_ref, w_ref, hval_ref, grad_ref,
    next_ref, grad_out_ref, ocean_ref, acc,
):
    step = pl.program_id(0)

    @pl.when(step == 0)
    def _():
        def clear(i, carry):
            acc[i] = jnp.zeros(acc.shape[1:], acc.dtype)
            return carry

        lax.fori_loop(0, acc.shape[0], clear, 0)

    next_ref[...] = jnp.dot(
        hval_ref[...], mix_ref[...], preferred_element_type=jnp.float32
    ).astype(jnp.bfloat16)
    grad_out_ref[...] = grad_ref[...]
    for k in range(per):
        e = step * per + k
        product = jnp.dot(near_ref[slot_ref[e]], w_ref[k], preferred_element_type=jnp.float32)
        acc[src_ref[e]] += product

    @pl.when(step == pl.num_programs(0) - 1)
    def _():
        def finish(i, carry):
            total = jnp.where(mask_ref[pl.ds(i, 1), :] == 1, acc[i], 0.0)
            ocean_ref[i] = total.T.astype(jnp.bfloat16)
            return carry

        lax.fori_loop(0, acc.shape[0], finish, 0, unroll=2)


def whole(shape):
    return pl.BlockSpec(shape, lambda i, *_: (0,) * len(shape))


def shards(
    ocean_field, ocean_mask, remap_weight, source_tile, target_tile, dest_device,
    atm_state, kappa, mix, cotangent,
):
    devices = lax.axis_size("tile")
    me = lax.axis_index("tile")
    entries, tile, _ = remap_weight.shape
    channels = ocean_field.shape[1]
    ocn = ocean_field.shape[0] // tile
    rows = atm_state.shape[0]
    atm = rows // tile
    slots = SPAN * atm
    per = entries // STEPS
    dest = lax.dynamic_slice_in_dim(dest_device.reshape(-1), me * entries, entries)
    target = lax.dynamic_slice_in_dim(target_tile, me * entries, entries)
    slot = lax.rem(dest - me + WIN + devices, devices) * atm + target
    mask = ocean_mask.reshape(ocn, tile)
    params = functools.partial(pltpu.CompilerParams, vmem_limit_bytes=VMEM_BYTES)

    part = pl.pallas_call(
        functools.partial(forward_kernel, per),
        out_shape=jax.ShapeDtypeStruct((slots, tile, channels), jnp.bfloat16),
        grid_spec=pltpu.PrefetchScalarGridSpec(
            num_scalar_prefetch=2,
            grid=(STEPS,),
            in_specs=[
                whole((ocn, tile, channels)),
                whole((ocn, tile)),
                pl.BlockSpec((per, tile, tile), lambda i, *_: (i, 0, 0)),
            ],
            out_specs=whole((slots, tile, channels)),
            scratch_shapes=[
                pltpu.VMEM((slots, tile, channels), jnp.float32),
                pltpu.VMEM((ocn, tile, channels), jnp.bfloat16),
            ],
        ),
        compiler_params=params(),
        name="remap_forward",
    )(source_tile, slot, ocean_field.reshape(ocn, tile, channels), mask, remap_weight)

    vmem = pl.BlockSpec(memory_space=pltpu.VMEM)
    hbm = pl.BlockSpec(memory_space=pl.ANY)
    f32 = lambda *shape: pltpu.VMEM(shape, jnp.float32)
    near, grad, hval = pl.pallas_call(
        functools.partial(middle_kernel, devices, tile),
        out_shape=(
            jax.ShapeDtypeStruct((SPAN, rows, channels), jnp.bfloat16),
            jax.ShapeDtypeStruct((rows, channels), jnp.bfloat16),
            jax.ShapeDtypeStruct((rows, channels), jnp.bfloat16),
        ),
        in_specs=[hbm, vmem, vmem, vmem, vmem],
        out_specs=(hbm, vmem, vmem),
        scratch_shapes=[
            pltpu.VMEM((SPAN, rows, channels), jnp.bfloat16),
            f32(rows + 2 * HALO, channels),
            f32(rows + 2 * HALO, channels),
            f32(rows, channels),
            f32(rows, channels),
            f32(HALO, channels),
            f32(HALO, channels),
            f32(HALO, channels),
            f32(HALO, channels),
            pltpu.VMEM((rows, channels), jnp.bfloat16),
            pltpu.SemaphoreType.DMA((SPAN,)),
            pltpu.SemaphoreType.DMA((SPAN,)),
            pltpu.SemaphoreType.DMA((4,)),
            pltpu.SemaphoreType.DMA((4,)),
            pltpu.SemaphoreType.DMA((3, SPAN)),
            pltpu.SemaphoreType.DMA((3, SPAN)),
            pltpu.SemaphoreType.DMA((2,)),
        ],
        compiler_params=params(collective_id=0, has_side_effects=True),
        name="exchange_and_step",
    )(part.reshape(SPAN, rows, channels), atm_state, kappa, mix, cotangent)

    cut = pl.BlockSpec((rows // STEPS, channels), lambda i, *_: (i, 0))
    atm_next, atm_grad, ocean_grad = pl.pallas_call(
        functools.partial(adjoint_kernel, per),
        out_shape=(
            jax.ShapeDtypeStruct((rows, channels), jnp.bfloat16),
            jax.ShapeDtypeStruct((rows, channels), jnp.bfloat16),
            jax.ShapeDtypeStruct((ocn, tile, channels), jnp.bfloat16),
        ),
        grid_spec=pltpu.PrefetchScalarGridSpec(
            num_scalar_prefetch=2,
            grid=(STEPS,),
            in_specs=[
                whole((slots, tile, channels)),
                whole((ocn, tile)),
                whole((channels, channels)),
                pl.BlockSpec((per, tile, tile), lambda i, *_: (i, 0, 0)),
                cut,
                cut,
            ],
            out_specs=(cut, cut, whole((ocn, tile, channels))),
            scratch_shapes=[pltpu.VMEM((ocn, channels, tile), jnp.float32)],
        ),
        compiler_params=params(),
        name="remap_adjoint",
    )(
        source_tile, slot, near.reshape(slots, tile, channels), mask, mix, remap_weight,
        hval, grad,
    )
    return atm_next, atm_grad, ocean_grad.reshape(ocn * tile, channels)


def solution(mesh):
    both = P(("ens", "tile"), None)
    return jax.shard_map(
        shards,
        mesh=mesh,
        in_specs=(
            both, P("tile"), P("tile", None, None), P("tile"), P(), P(),
            both, P("tile", None), P(), both,
        ),
        out_specs=(both, both, both),
        check_vma=False,
    )
```

```python
import functools

import jax
import jax.numpy as jnp
from jax import lax
from jax.experimental import pallas as pl
from jax.experimental.pallas import tpu as pltpu
from jax.sharding import PartitionSpec as P

WIN = 4
SPAN = 2 * WIN + 1
HALO = 8
STEPS = 16
VMEM_BYTES = 56 * 1024 * 1024


def diagonal(row, size):
    eye = lax.broadcasted_iota(jnp.int32, (size, size), 0) == lax.broadcasted_iota(
        jnp.int32, (size, size), 1
    )
    return jnp.where(eye, jnp.broadcast_to(row, (size, size)), 0).astype(jnp.bfloat16)


def forward_kernel(per, src_ref, slot_ref, ocean_ref, mask_ref, w_ref, out_ref, acc, xm):
    step = pl.program_id(0)
    tile = w_ref.shape[1]

    @pl.when(step == 0)
    def _():
        def clear(i, carry):
            acc[i] = jnp.zeros(acc.shape[1:], acc.dtype)
            return carry

        lax.fori_loop(0, acc.shape[0], clear, 0)

        def mask_tile(i, carry):
            keep = jnp.where(mask_ref[pl.ds(i, 1), :] == 1, 1.0, 0.0)
            xm[i] = jnp.dot(
                diagonal(keep, tile), ocean_ref[i], preferred_element_type=jnp.float32
            ).astype(jnp.bfloat16)
            return carry

        lax.fori_loop(0, xm.shape[0], mask_tile, 0, unroll=4)

    for k in range(per):
        e = step * per + k
        product = jnp.dot(w_ref[k], xm[src_ref[e]], preferred_element_type=jnp.float32)
        acc[slot_ref[e]] += product

    @pl.when(step == pl.num_programs(0) - 1)
    def _():
        def narrow(i, carry):
            out_ref[i] = acc[i].astype(out_ref.dtype)
            return carry

        lax.fori_loop(0, acc.shape[0], narrow, 0, unroll=4)


def middle_kernel(
    devices, tile, part, atm_ref, kappa_ref, mix_ref, cot_ref,
    near, grad_ref, hval_ref,
    even, odd, recv, fpad, wpad, gs, gt, lo, hi, lo2, hi2, own,
    local_sem, osend, orecv, psend, precv, hsend, hrecv, gsend, grecv, xsend, xrecv,
):
    me = lax.axis_index("tile")
    core = lax.rem(me, 2)
    partner = me + 1 - 2 * core
    rows = atm_ref.shape[0]
    tiles = rows // tile
    far, alone = 4 - 4 * core, 4 * core

    def at(offset):
        return lax.rem(me + offset + devices, devices)

    def copy_to(src, dst, ssem, rsem, device):
        return pltpu.make_async_remote_copy(
            src_ref=src, dst_ref=dst, send_sem=ssem, recv_sem=rsem,
            device_id={"tile": device}, device_id_type=pl.DeviceIdType.MESH,
        )

    loads = [
        pltpu.make_async_copy(part.at[2 * m], even.at[m], local_sem.at[m]) for m in range(5)
    ]
    for c in loads:
        c.start()

    barrier = pltpu.get_barrier_semaphore()
    for o in (1, -1, 2, -2, 4, -4):
        pl.semaphore_signal(
            barrier, inc=1, device_id={"tile": at(o)}, device_id_type=pl.DeviceIdType.MESH
        )
    pl.semaphore_wait(barrier, 6)

    def swap(j):
        return copy_to(part.at[2 * j + 1], odd.at[j], osend.at[j], orecv.at[j], partner)

    def ship(m):
        return copy_to(even.at[m], recv.at[m], psend.at[m], precv.at[m], at(2 * m - 4))

    for j in (3 * core, 1 - core, 3 - core, 2 - core):
        swap(j).start()
    for c in loads:
        c.wait()
    ship(alone).start()

    def combine(m):
        j = m - 1 + core
        swap(j).wait_recv()

        def body(i, carry):
            at_rows = pl.ds(pl.multiple_of(i * tile, tile), tile)
            total = even[m, at_rows, :].astype(jnp.float32)
            total = total + odd[j, at_rows, :].astype(jnp.float32)
            even[m, at_rows, :] = total.astype(jnp.bfloat16)
            return carry

        lax.fori_loop(0, tiles, body, 0, unroll=2)

    for m in (far, 1, 3):
        combine(m)
        ship(m).start()
    swap(1 + core).wait_recv()

    def adjoint_mix(i, carry):
        at_rows = pl.ds(pl.multiple_of(i * tile, tile), tile)
        gt[at_rows, :] = lax.dot_general(
            cot_ref[at_rows, :], mix_ref[...], (((1,), (1,)), ((), ())),
            preferred_element_type=jnp.float32,
        )
        total = atm_ref[at_rows, :].astype(jnp.float32)
        total = total + even[2, at_rows, :].astype(jnp.float32)
        total = total + odd[1 + core, at_rows, :].astype(jnp.float32)
        fpad[pl.ds(pl.multiple_of(i * tile + HALO, HALO), tile), :] = total
        return carry

    lax.fori_loop(0, tiles, adjoint_mix, 0, unroll=2)

    def add_parts(slots):
        def body(i, carry):
            at_rows = pl.ds(pl.multiple_of(i * tile, tile), tile)
            pad_rows = pl.ds(pl.multiple_of(i * tile + HALO, HALO), tile)
            total = fpad[pad_rows, :]
            for slot in slots:
                total = total + recv[slot, at_rows, :].astype(jnp.float32)
            fpad[pad_rows, :] = total
            return carry

        lax.fori_loop(0, tiles, body, 0, unroll=2)

    for pair in ((1, 3), (0, 4)):
        for m in pair:
            ship(m).wait_recv()
        add_parts(pair)

    def edges(pad, low, high, k):
        up = copy_to(pad.at[pl.ds(rows, HALO), :], low, hsend.at[k], hrecv.at[k], at(1))
        down = copy_to(pad.at[pl.ds(HALO, HALO), :], high, hsend.at[k + 1], hrecv.at[k + 1], at(-1))
        return up, down

    def window(pad, i):
        w = pad[pl.ds(pl.multiple_of(i * tile, tile), tile + 2 * HALO), :]
        return w[HALO - 1 : HALO - 1 + tile], w[HALO : HALO + tile], w[HALO + 1 : HALO + 1 + tile]

    fwd_edges = edges(fpad, lo, hi, 0)
    for c in fwd_edges:
        c.start()

    def primal(i, carry):
        at_rows = pl.ds(pl.multiple_of(i * tile, tile), tile)
        before, x, after = window(fpad, i)
        kappa = kappa_ref[at_rows, :]
        th = jnp.tanh(x + kappa * (before + after - 2.0 * x))
        hval_ref[at_rows, :] = th.astype(jnp.bfloat16)
        g = gt[at_rows, :] * (1.0 - th * th)
        gs[at_rows, :] = g
        wpad[pl.ds(pl.multiple_of(i * tile + HALO, HALO), tile), :] = kappa * g
        return carry

    lax.fori_loop(1, tiles - 1, primal, 0)
    for c in fwd_edges:
        c.wait()
    fpad[0:HALO, :] = lo[...]
    fpad[rows + HALO : rows + 2 * HALO, :] = hi[...]
    lax.fori_loop(0, 2, lambda j, c: primal(j * (tiles - 1), c), 0)

    adj_edges = edges(wpad, lo2, hi2, 2)
    for c in adj_edges:
        c.start()

    def adjoint(i, carry):
        at_rows = pl.ds(pl.multiple_of(i * tile, tile), tile)
        before, x, after = window(wpad, i)
        grad = gs[at_rows, :] + before + after - 2.0 * x
        grad_ref[at_rows, :] = grad.astype(jnp.bfloat16)
        own[at_rows, :] = grad.T.astype(jnp.bfloat16)
        return carry

    pieces = [(tile, rows - 2 * tile), (0, tile), (rows - tile, tile)]

    def grads(p, m):
        cut = pl.ds(pieces[p][0], pieces[p][1])
        return copy_to(
            own.at[cut, :], near.at[2 * m, cut, :], gsend.at[p, m], grecv.at[p, m], at(4 - 2 * m)
        )

    def hand(p, m, src):
        cut = pl.ds(pieces[p][0], pieces[p][1])
        j = m - 1 + core
        return copy_to(
            src, near.at[2 * j + 1, cut, :], xsend.at[p, j], xrecv.at[p, j], partner
        )

    def own_cut(p):
        return own.at[pl.ds(pieces[p][0], pieces[p][1]), :]

    def near_cut(p, m):
        return near.at[2 * m, pl.ds(pieces[p][0], pieces[p][1]), :]

    lax.fori_loop(1, tiles - 1, adjoint, 0)
    order = (0, 4, 1, 3)
    for m in order:
        grads(0, m).start()
    hand(0, 2, own_cut(0)).start()
    for c in adj_edges:
        c.wait()
    wpad[0:HALO, :] = lo2[...]
    wpad[rows + HALO : rows + 2 * HALO, :] = hi2[...]
    lax.fori_loop(0, 2, lambda j, c: adjoint(j * (tiles - 1), c), 0)
    for p in (1, 2):
        for m in order:
            grads(p, m).start()
        hand(p, 2, own_cut(p)).start()
    keep = pltpu.make_async_copy(own, near.at[2 * 2], local_sem.at[5])
    keep.start()
    for m in (1, 3, far):
        for p in range(3):
            grads(p, m).wait_recv()
            hand(p, m, near_cut(p, m)).start()
    for p in range(3):
        grads(p, alone).wait_recv()
    keep.wait()
    for p in range(3):
        for j in range(4):
            out = hand(p, j + 1 - core, own_cut(p))
            out.wait_send()
            out.wait_recv()
        for m in order:
            grads(p, m).wait_send()
    for j in range(4):
        swap(j).wait_send()
    for m in order:
        ship(m).wait_send()


def adjoint_kernel(
    per, src_ref, slot_ref, near_ref, mask_ref, mix_ref, w_ref, hval_ref, grad_ref,
    next_ref, grad_out_ref, ocean_ref, acc,
):
    step = pl.program_id(0)

    @pl.when(step == 0)
    def _():
        def clear(i, carry):
            acc[i] = jnp.zeros(acc.shape[1:], acc.dtype)
            return carry

        lax.fori_loop(0, acc.shape[0], clear, 0)

    next_ref[...] = jnp.dot(
        hval_ref[...], mix_ref[...], preferred_element_type=jnp.float32
    ).astype(jnp.bfloat16)
    grad_out_ref[...] = grad_ref[...]
    for k in range(per):
        e = step * per + k
        product = jnp.dot(near_ref[slot_ref[e]], w_ref[k], preferred_element_type=jnp.float32)
        acc[src_ref[e]] += product

    @pl.when(step == pl.num_programs(0) - 1)
    def _():
        def finish(i, carry):
            total = jnp.where(mask_ref[pl.ds(i, 1), :] == 1, acc[i], 0.0)
            ocean_ref[i] = total.T.astype(jnp.bfloat16)
            return carry

        lax.fori_loop(0, acc.shape[0], finish, 0, unroll=2)


def whole(shape):
    return pl.BlockSpec(shape, lambda i, *_: (0,) * len(shape))


def shards(
    ocean_field, ocean_mask, remap_weight, source_tile, target_tile, dest_device,
    atm_state, kappa, mix, cotangent,
):
    devices = lax.axis_size("tile")
    me = lax.axis_index("tile")
    entries, tile, _ = remap_weight.shape
    channels = ocean_field.shape[1]
    ocn = ocean_field.shape[0] // tile
    rows = atm_state.shape[0]
    atm = rows // tile
    slots = SPAN * atm
    per = entries // STEPS
    dest = lax.dynamic_slice_in_dim(dest_device.reshape(-1), me * entries, entries)
    target = lax.dynamic_slice_in_dim(target_tile, me * entries, entries)
    slot = lax.rem(dest - me + WIN + devices, devices) * atm + target
    mask = ocean_mask.reshape(ocn, tile)
    params = functools.partial(pltpu.CompilerParams, vmem_limit_bytes=VMEM_BYTES)

    part = pl.pallas_call(
        functools.partial(forward_kernel, per),
        out_shape=jax.ShapeDtypeStruct((slots, tile, channels), jnp.bfloat16),
        grid_spec=pltpu.PrefetchScalarGridSpec(
            num_scalar_prefetch=2,
            grid=(STEPS,),
            in_specs=[
                whole((ocn, tile, channels)),
                whole((ocn, tile)),
                pl.BlockSpec((per, tile, tile), lambda i, *_: (i, 0, 0)),
            ],
            out_specs=whole((slots, tile, channels)),
            scratch_shapes=[
                pltpu.VMEM((slots, tile, channels), jnp.float32),
                pltpu.VMEM((ocn, tile, channels), jnp.bfloat16),
            ],
        ),
        compiler_params=params(),
        name="remap_forward",
    )(source_tile, slot, ocean_field.reshape(ocn, tile, channels), mask, remap_weight)

    vmem = pl.BlockSpec(memory_space=pltpu.VMEM)
    hbm = pl.BlockSpec(memory_space=pl.ANY)
    f32 = lambda *shape: pltpu.VMEM(shape, jnp.float32)
    near, grad, hval = pl.pallas_call(
        functools.partial(middle_kernel, devices, tile),
        out_shape=(
            jax.ShapeDtypeStruct((SPAN, rows, channels), jnp.bfloat16),
            jax.ShapeDtypeStruct((rows, channels), jnp.bfloat16),
            jax.ShapeDtypeStruct((rows, channels), jnp.bfloat16),
        ),
        in_specs=[hbm, vmem, vmem, vmem, vmem],
        out_specs=(hbm, vmem, vmem),
        scratch_shapes=[
            pltpu.VMEM((5, rows, channels), jnp.bfloat16),
            pltpu.VMEM((4, rows, channels), jnp.bfloat16),
            pltpu.VMEM((5, rows, channels), jnp.bfloat16),
            f32(rows + 2 * HALO, channels),
            f32(rows + 2 * HALO, channels),
            f32(rows, channels),
            f32(rows, channels),
            f32(HALO, channels),
            f32(HALO, channels),
            f32(HALO, channels),
            f32(HALO, channels),
            pltpu.VMEM((rows, channels), jnp.bfloat16),
            pltpu.SemaphoreType.DMA((6,)),
            pltpu.SemaphoreType.DMA((4,)),
            pltpu.SemaphoreType.DMA((4,)),
            pltpu.SemaphoreType.DMA((5,)),
            pltpu.SemaphoreType.DMA((5,)),
            pltpu.SemaphoreType.DMA((4,)),
            pltpu.SemaphoreType.DMA((4,)),
            pltpu.SemaphoreType.DMA((3, 5)),
            pltpu.SemaphoreType.DMA((3, 5)),
            pltpu.SemaphoreType.DMA((3, 4)),
            pltpu.SemaphoreType.DMA((3, 4)),
        ],
        compiler_params=params(collective_id=0, has_side_effects=True),
        name="exchange_and_step",
    )(part.reshape(SPAN, rows, channels), atm_state, kappa, mix, cotangent)

    cut = pl.BlockSpec((rows // STEPS, channels), lambda i, *_: (i, 0))
    atm_next, atm_grad, ocean_grad = pl.pallas_call(
        functools.partial(adjoint_kernel, per),
        out_shape=(
            jax.ShapeDtypeStruct((rows, channels), jnp.bfloat16),
            jax.ShapeDtypeStruct((rows, channels), jnp.bfloat16),
            jax.ShapeDtypeStruct((ocn, tile, channels), jnp.bfloat16),
        ),
        grid_spec=pltpu.PrefetchScalarGridSpec(
            num_scalar_prefetch=2,
            grid=(STEPS,),
            in_specs=[
                whole((slots, tile, channels)),
                whole((ocn, tile)),
                whole((channels, channels)),
                pl.BlockSpec((per, tile, tile), lambda i, *_: (i, 0, 0)),
                cut,
                cut,
            ],
            out_specs=(cut, cut, whole((ocn, tile, channels))),
            scratch_shapes=[pltpu.VMEM((ocn, channels, tile), jnp.float32)],
        ),
        compiler_params=params(),
        name="remap_adjoint",
    )(
        source_tile, slot, near.reshape(slots, tile, channels), mask, mix, remap_weight,
        hval, grad,
    )
    return atm_next, atm_grad, ocean_grad.reshape(ocn * tile, channels)


def solution(mesh):
    both = P(("ens", "tile"), None)
    return jax.shard_map(
        shards,
        mesh=mesh,
        in_specs=(
            both, P("tile"), P("tile", None, None), P("tile"), P(), P(),
            both, P("tile", None), P(), both,
        ),
        out_specs=(both, both, both),
        check_vma=False,
    )
```

```python
import functools

import jax
import jax.numpy as jnp
from jax import lax
from jax.experimental import pallas as pl
from jax.experimental.pallas import tpu as pltpu
from jax.sharding import PartitionSpec as P

WIN = 4
SPAN = 2 * WIN + 1
HALO = 8
STEPS = 16
VMEM_BYTES = 56 * 1024 * 1024


def diagonal(row, size):
    eye = lax.broadcasted_iota(jnp.int32, (size, size), 0) == lax.broadcasted_iota(
        jnp.int32, (size, size), 1
    )
    return jnp.where(eye, jnp.broadcast_to(row, (size, size)), 0).astype(jnp.bfloat16)


def forward_kernel(per, src_ref, slot_ref, ocean_ref, mask_ref, w_ref, out_ref, acc, xm):
    step = pl.program_id(0)
    tile = w_ref.shape[1]

    @pl.when(step == 0)
    def _():
        def clear(i, carry):
            acc[i] = jnp.zeros(acc.shape[1:], acc.dtype)
            return carry

        lax.fori_loop(0, acc.shape[0], clear, 0)

        def mask_tile(i, carry):
            keep = jnp.where(mask_ref[pl.ds(i, 1), :] == 1, 1.0, 0.0)
            xm[i] = jnp.dot(
                diagonal(keep, tile), ocean_ref[i], preferred_element_type=jnp.float32
            ).astype(jnp.bfloat16)
            return carry

        lax.fori_loop(0, xm.shape[0], mask_tile, 0, unroll=4)

    for k in range(per):
        e = step * per + k
        product = jnp.dot(w_ref[k], xm[src_ref[e]], preferred_element_type=jnp.float32)
        acc[slot_ref[e]] += product

    @pl.when(step == pl.num_programs(0) - 1)
    def _():
        def narrow(i, carry):
            out_ref[i] = acc[i].astype(out_ref.dtype)
            return carry

        lax.fori_loop(0, acc.shape[0], narrow, 0, unroll=4)


def middle_kernel(
    devices, tile, part, atm_ref, kappa_ref, mix_ref, cot_ref,
    near, grad_ref, hval_ref,
    even, odd, recv, relayed, fpad, wpad, gs, gt, lo, hi, lo2, hi2, own,
    local_sem, osend, orecv, psend, precv, hsend, hrecv, gsend, grecv, xsend, xrecv, rsem,
):
    me = lax.axis_index("tile")
    core = lax.rem(me, 2)
    partner = me + 1 - 2 * core
    rows = atm_ref.shape[0]
    tiles = rows // tile
    side = lax.rem(me // 2, 2)
    across = lax.rem(me + 2 - 4 * side + devices, devices)
    far = 4 - 4 * core
    direct, passed, joined, plain = 3 - 2 * side, 1 + 2 * side, 4 - 4 * side, 4 * side

    def at(offset):
        return lax.rem(me + offset + devices, devices)

    def copy_to(src, dst, ssem, rsem, device):
        return pltpu.make_async_remote_copy(
            src_ref=src, dst_ref=dst, send_sem=ssem, recv_sem=rsem,
            device_id={"tile": device}, device_id_type=pl.DeviceIdType.MESH,
        )

    loads = [
        pltpu.make_async_copy(part.at[2 * m], even.at[m], local_sem.at[m]) for m in range(5)
    ]
    for c in loads:
        c.start()

    barrier = pltpu.get_barrier_semaphore()
    for o in (1, -1, 2, -2, 4, -4):
        pl.semaphore_signal(
            barrier, inc=1, device_id={"tile": at(o)}, device_id_type=pl.DeviceIdType.MESH
        )
    pl.semaphore_wait(barrier, 6)

    def swap(j):
        return copy_to(part.at[2 * j + 1], odd.at[j], osend.at[j], orecv.at[j], partner)

    def ship(m):
        return copy_to(even.at[m], recv.at[m], psend.at[m], precv.at[m], at(2 * m - 4))

    for j in (passed - core, 3 * core, direct - core, 2 - core):
        swap(j).start()
    for c in loads:
        c.wait()

    def combine(m):
        j = m - 1 + core
        swap(j).wait_recv()

        def body(i, carry):
            at_rows = pl.ds(pl.multiple_of(i * tile, tile), tile)
            total = even[m, at_rows, :].astype(jnp.float32)
            total = total + odd[j, at_rows, :].astype(jnp.float32)
            even[m, at_rows, :] = total.astype(jnp.bfloat16)
            return carry

        lax.fori_loop(0, tiles, body, 0, unroll=2)

    add_on = copy_to(even.at[passed], relayed, rsem.at[0], rsem.at[1], across)
    combine(passed)
    add_on.start()
    combine(far)
    ship(plain).start()
    combine(direct)
    ship(direct).start()
    swap(1 + core).wait_recv()

    def adjoint_mix(i, carry):
        at_rows = pl.ds(pl.multiple_of(i * tile, tile), tile)
        gt[at_rows, :] = lax.dot_general(
            cot_ref[at_rows, :], mix_ref[...], (((1,), (1,)), ((), ())),
            preferred_element_type=jnp.float32,
        )
        total = atm_ref[at_rows, :].astype(jnp.float32)
        total = total + even[2, at_rows, :].astype(jnp.float32)
        total = total + odd[1 + core, at_rows, :].astype(jnp.float32)
        fpad[pl.ds(pl.multiple_of(i * tile + HALO, HALO), tile), :] = total
        return carry

    lax.fori_loop(0, tiles, adjoint_mix, 0, unroll=2)

    def add_parts(slots):
        def body(i, carry):
            at_rows = pl.ds(pl.multiple_of(i * tile, tile), tile)
            pad_rows = pl.ds(pl.multiple_of(i * tile + HALO, HALO), tile)
            total = fpad[pad_rows, :]
            for slot in slots:
                total = total + recv[slot, at_rows, :].astype(jnp.float32)
            fpad[pad_rows, :] = total
            return carry

        lax.fori_loop(0, tiles, body, 0, unroll=2)

    add_on.wait_recv()

    def join(i, carry):
        at_rows = pl.ds(pl.multiple_of(i * tile, tile), tile)
        total = even[joined, at_rows, :].astype(jnp.float32)
        total = total + relayed[at_rows, :].astype(jnp.float32)
        even[joined, at_rows, :] = total.astype(jnp.bfloat16)
        return carry

    lax.fori_loop(0, tiles, join, 0, unroll=2)
    ship(joined).start()
    ship(plain).wait_recv()
    add_parts([plain])
    ship(passed).wait_recv()
    add_parts([passed])
    ship(joined).wait_recv()
    add_parts([joined])

    def edges(pad, low, high, k):
        up = copy_to(pad.at[pl.ds(rows, HALO), :], low, hsend.at[k], hrecv.at[k], at(1))
        down = copy_to(pad.at[pl.ds(HALO, HALO), :], high, hsend.at[k + 1], hrecv.at[k + 1], at(-1))
        return up, down

    def window(pad, i):
        w = pad[pl.ds(pl.multiple_of(i * tile, tile), tile + 2 * HALO), :]
        return w[HALO - 1 : HALO - 1 + tile], w[HALO : HALO + tile], w[HALO + 1 : HALO + 1 + tile]

    fwd_edges = edges(fpad, lo, hi, 0)
    for c in fwd_edges:
        c.start()

    def primal(i, carry):
        at_rows = pl.ds(pl.multiple_of(i * tile, tile), tile)
        before, x, after = window(fpad, i)
        kappa = kappa_ref[at_rows, :]
        th = jnp.tanh(x + kappa * (before + after - 2.0 * x))
        hval_ref[at_rows, :] = th.astype(jnp.bfloat16)
        g = gt[at_rows, :] * (1.0 - th * th)
        gs[at_rows, :] = g
        wpad[pl.ds(pl.multiple_of(i * tile + HALO, HALO), tile), :] = kappa * g
        return carry

    lax.fori_loop(1, tiles - 1, primal, 0)
    for c in fwd_edges:
        c.wait()
    fpad[0:HALO, :] = lo[...]
    fpad[rows + HALO : rows + 2 * HALO, :] = hi[...]
    lax.fori_loop(0, 2, lambda j, c: primal(j * (tiles - 1), c), 0)

    adj_edges = edges(wpad, lo2, hi2, 2)
    for c in adj_edges:
        c.start()

    def adjoint(i, carry):
        at_rows = pl.ds(pl.multiple_of(i * tile, tile), tile)
        before, x, after = window(wpad, i)
        grad = gs[at_rows, :] + before + after - 2.0 * x
        grad_ref[at_rows, :] = grad.astype(jnp.bfloat16)
        own[at_rows, :] = grad.T.astype(jnp.bfloat16)
        return carry

    half = tiles // 2 * tile
    pieces = [(tile, half - tile), (half, rows - tile - half), (0, tile), (rows - tile, tile)]

    def grads(p, m):
        cut = pl.ds(pieces[p][0], pieces[p][1])
        return copy_to(
            own.at[cut, :], near.at[2 * m, cut, :], gsend.at[p, m], grecv.at[p, m], at(4 - 2 * m)
        )

    def hand(p, m, src):
        cut = pl.ds(pieces[p][0], pieces[p][1])
        j = m - 1 + core
        return copy_to(
            src, near.at[2 * j + 1, cut, :], xsend.at[p, j], xrecv.at[p, j], partner
        )

    def relay(p):
        cut = pl.ds(pieces[p][0], pieces[p][1])
        return copy_to(
            near_cut(p, joined), near.at[2 * direct, cut, :],
            gsend.at[p, direct], grecv.at[p, direct], across,
        )

    def own_cut(p):
        return own.at[pl.ds(pieces[p][0], pieces[p][1]), :]

    def near_cut(p, m):
        return near.at[2 * m, pl.ds(pieces[p][0], pieces[p][1]), :]

    lax.fori_loop(1, tiles - 1, adjoint, 0)
    for p in (0, 1):
        grads(p, joined).start()
        grads(p, passed).start()
        hand(p, 2, own_cut(p)).start()
    for c in adj_edges:
        c.wait()
    wpad[0:HALO, :] = lo2[...]
    wpad[rows + HALO : rows + 2 * HALO, :] = hi2[...]
    lax.fori_loop(0, 2, lambda j, c: adjoint(j * (tiles - 1), c), 0)
    for p in (2, 3):
        grads(p, joined).start()
        grads(p, passed).start()
        hand(p, 2, own_cut(p)).start()
    keep = pltpu.make_async_copy(own, near.at[2 * 2], local_sem.at[5])
    keep.start()
    for p in range(4):
        grads(p, joined).wait_recv()
        relay(p).start()
        grads(p, joined).wait_send()
        grads(p, plain).start()
    for p in range(4):
        grads(p, direct).wait_recv()
        hand(p, direct, near_cut(p, direct)).start()
    for p in range(4):
        grads(p, plain).wait_recv()
        hand(p, far, near_cut(p, far)).start()
    for p in range(4):
        grads(p, passed).wait_recv()
        hand(p, passed, near_cut(p, passed)).start()
    keep.wait()
    for p in range(4):
        for j in range(4):
            out = hand(p, j + 1 - core, own_cut(p))
            out.wait_send()
            out.wait_recv()
        grads(p, passed).wait_send()
        grads(p, plain).wait_send()
        relay(p).wait_send()
    for j in range(4):
        swap(j).wait_send()
    for m in (plain, direct, joined):
        ship(m).wait_send()
    add_on.wait_send()


def adjoint_kernel(
    per, src_ref, slot_ref, near_ref, mask_ref, mix_ref, w_ref, hval_ref, grad_ref,
    next_ref, grad_out_ref, ocean_ref, acc,
):
    step = pl.program_id(0)

    @pl.when(step == 0)
    def _():
        def clear(i, carry):
            acc[i] = jnp.zeros(acc.shape[1:], acc.dtype)
            return carry

        lax.fori_loop(0, acc.shape[0], clear, 0)

    next_ref[...] = jnp.dot(
        hval_ref[...], mix_ref[...], preferred_element_type=jnp.float32
    ).astype(jnp.bfloat16)
    grad_out_ref[...] = grad_ref[...]
    for k in range(per):
        e = step * per + k
        product = jnp.dot(near_ref[slot_ref[e]], w_ref[k], preferred_element_type=jnp.float32)
        acc[src_ref[e]] += product

    @pl.when(step == pl.num_programs(0) - 1)
    def _():
        def finish(i, carry):
            total = jnp.where(mask_ref[pl.ds(i, 1), :] == 1, acc[i], 0.0)
            ocean_ref[i] = total.T.astype(jnp.bfloat16)
            return carry

        lax.fori_loop(0, acc.shape[0], finish, 0, unroll=2)


def whole(shape):
    return pl.BlockSpec(shape, lambda i, *_: (0,) * len(shape))


def shards(
    ocean_field, ocean_mask, remap_weight, source_tile, target_tile, dest_device,
    atm_state, kappa, mix, cotangent,
):
    devices = lax.axis_size("tile")
    me = lax.axis_index("tile")
    entries, tile, _ = remap_weight.shape
    channels = ocean_field.shape[1]
    ocn = ocean_field.shape[0] // tile
    rows = atm_state.shape[0]
    atm = rows // tile
    slots = SPAN * atm
    per = entries // STEPS
    dest = lax.dynamic_slice_in_dim(dest_device.reshape(-1), me * entries, entries)
    target = lax.dynamic_slice_in_dim(target_tile, me * entries, entries)
    slot = lax.rem(dest - me + WIN + devices, devices) * atm + target
    mask = ocean_mask.reshape(ocn, tile)
    params = functools.partial(pltpu.CompilerParams, vmem_limit_bytes=VMEM_BYTES)

    part = pl.pallas_call(
        functools.partial(forward_kernel, per),
        out_shape=jax.ShapeDtypeStruct((slots, tile, channels), jnp.bfloat16),
        grid_spec=pltpu.PrefetchScalarGridSpec(
            num_scalar_prefetch=2,
            grid=(STEPS,),
            in_specs=[
                whole((ocn, tile, channels)),
                whole((ocn, tile)),
                pl.BlockSpec((per, tile, tile), lambda i, *_: (i, 0, 0)),
            ],
            out_specs=whole((slots, tile, channels)),
            scratch_shapes=[
                pltpu.VMEM((slots, tile, channels), jnp.float32),
                pltpu.VMEM((ocn, tile, channels), jnp.bfloat16),
            ],
        ),
        compiler_params=params(),
        name="remap_forward",
    )(source_tile, slot, ocean_field.reshape(ocn, tile, channels), mask, remap_weight)

    vmem = pl.BlockSpec(memory_space=pltpu.VMEM)
    hbm = pl.BlockSpec(memory_space=pl.ANY)
    f32 = lambda *shape: pltpu.VMEM(shape, jnp.float32)
    near, grad, hval = pl.pallas_call(
        functools.partial(middle_kernel, devices, tile),
        out_shape=(
            jax.ShapeDtypeStruct((SPAN, rows, channels), jnp.bfloat16),
            jax.ShapeDtypeStruct((rows, channels), jnp.bfloat16),
            jax.ShapeDtypeStruct((rows, channels), jnp.bfloat16),
        ),
        in_specs=[hbm, vmem, vmem, vmem, vmem],
        out_specs=(hbm, vmem, vmem),
        scratch_shapes=[
            pltpu.VMEM((5, rows, channels), jnp.bfloat16),
            pltpu.VMEM((4, rows, channels), jnp.bfloat16),
            pltpu.VMEM((5, rows, channels), jnp.bfloat16),
            pltpu.VMEM((rows, channels), jnp.bfloat16),
            f32(rows + 2 * HALO, channels),
            f32(rows + 2 * HALO, channels),
            f32(rows, channels),
            f32(rows, channels),
            f32(HALO, channels),
            f32(HALO, channels),
            f32(HALO, channels),
            f32(HALO, channels),
            pltpu.VMEM((rows, channels), jnp.bfloat16),
            pltpu.SemaphoreType.DMA((6,)),
            pltpu.SemaphoreType.DMA((4,)),
            pltpu.SemaphoreType.DMA((4,)),
            pltpu.SemaphoreType.DMA((5,)),
            pltpu.SemaphoreType.DMA((5,)),
            pltpu.SemaphoreType.DMA((4,)),
            pltpu.SemaphoreType.DMA((4,)),
            pltpu.SemaphoreType.DMA((4, 5)),
            pltpu.SemaphoreType.DMA((4, 5)),
            pltpu.SemaphoreType.DMA((4, 4)),
            pltpu.SemaphoreType.DMA((4, 4)),
            pltpu.SemaphoreType.DMA((2,)),
        ],
        compiler_params=params(collective_id=0, has_side_effects=True),
        name="exchange_and_step",
    )(part.reshape(SPAN, rows, channels), atm_state, kappa, mix, cotangent)

    cut = pl.BlockSpec((rows // STEPS, channels), lambda i, *_: (i, 0))
    atm_next, atm_grad, ocean_grad = pl.pallas_call(
        functools.partial(adjoint_kernel, per),
        out_shape=(
            jax.ShapeDtypeStruct((rows, channels), jnp.bfloat16),
            jax.ShapeDtypeStruct((rows, channels), jnp.bfloat16),
            jax.ShapeDtypeStruct((ocn, tile, channels), jnp.bfloat16),
        ),
        grid_spec=pltpu.PrefetchScalarGridSpec(
            num_scalar_prefetch=2,
            grid=(STEPS,),
            in_specs=[
                whole((slots, tile, channels)),
                whole((ocn, tile)),
                whole((channels, channels)),
                pl.BlockSpec((per, tile, tile), lambda i, *_: (i, 0, 0)),
                cut,
                cut,
            ],
            out_specs=(cut, cut, whole((ocn, tile, channels))),
            scratch_shapes=[pltpu.VMEM((ocn, channels, tile), jnp.float32)],
        ),
        compiler_params=params(),
        name="remap_adjoint",
    )(
        source_tile, slot, near.reshape(slots, tile, channels), mask, mix, remap_weight,
        hval, grad,
    )
    return atm_next, atm_grad, ocean_grad.reshape(ocn * tile, channels)


def solution(mesh):
    both = P(("ens", "tile"), None)
    return jax.shard_map(
        shards,
        mesh=mesh,
        in_specs=(
            both, P("tile"), P("tile", None, None), P("tile"), P(), P(),
            both, P("tile", None), P(), both,
        ),
        out_specs=(both, both, both),
        check_vma=False,
    )
```

```python
import functools

import jax
import jax.numpy as jnp
from jax import lax
from jax.experimental import pallas as pl
from jax.experimental.pallas import tpu as pltpu
from jax.sharding import PartitionSpec as P

WIN = 4
SPAN = 2 * WIN + 1
HALO = 8
CHUNKS = 4
VMEM_BYTES = 56 * 1024 * 1024


def diagonal(row, size):
    eye = lax.broadcasted_iota(jnp.int32, (size, size), 0) == lax.broadcasted_iota(
        jnp.int32, (size, size), 1
    )
    return jnp.where(eye, jnp.broadcast_to(row, (size, size)), 0).astype(jnp.bfloat16)


def fetch_all(w_hbm, wbuf, sems):
    per = w_hbm.shape[0] // CHUNKS

    def fetch(c):
        cut = pl.ds(c * per, per)
        return pltpu.make_async_copy(w_hbm.at[cut], wbuf.at[cut], sems.at[c])

    for c in range(CHUNKS):
        fetch(c).start()
    return fetch, per


def clear_all(acc):
    def clear(i, carry):
        acc[i] = jnp.zeros(acc.shape[1:], acc.dtype)
        return carry

    lax.fori_loop(0, acc.shape[0], clear, 0, unroll=4)


def forward_kernel(src_ref, slot_ref, ocean_ref, mask_ref, w_hbm, out_hbm, acc, xm, wbuf, obuf, sems, osems):
    tile = w_hbm.shape[1]
    fetch, per = fetch_all(w_hbm, wbuf, sems)
    clear_all(acc)

    def mask_tile(i, carry):
        keep = jnp.where(mask_ref[pl.ds(i, 1), :] == 1, 1.0, 0.0)
        xm[i] = jnp.dot(
            diagonal(keep, tile), ocean_ref[i], preferred_element_type=jnp.float32
        ).astype(jnp.bfloat16)
        return carry

    lax.fori_loop(0, xm.shape[0], mask_tile, 0, unroll=8)

    def block(c, carry):
        fetch(c).wait()
        for k in range(per):
            e = c * per + k
            product = jnp.dot(wbuf[e], xm[src_ref[e]], preferred_element_type=jnp.float32)
            acc[slot_ref[e]] += product
        return carry

    lax.fori_loop(0, CHUNKS, block, 0)
    group = acc.shape[0] // SPAN

    def put(o):
        cut = pl.ds(o * group, group)
        return pltpu.make_async_copy(obuf.at[cut], out_hbm.at[cut], osems.at[o])

    def narrow(o, carry):
        for t in range(group):
            obuf[o * group + t] = acc[o * group + t].astype(obuf.dtype)
        put(o).start()
        return carry

    lax.fori_loop(0, SPAN, narrow, 0)
    for o in range(SPAN):
        put(o).wait()


def middle_kernel(
    devices, tile, part, atm_ref, kappa_ref, mix_ref, cot_ref,
    near, grad_ref, hval_ref,
    even, odd, recv, relayed, fpad, wpad, gs, gt, lo, hi, lo2, hi2, own,
    local_sem, osend, orecv, psend, precv, hsend, hrecv, gsend, grecv, xsend, xrecv, rsem,
):
    me = lax.axis_index("tile")
    core = lax.rem(me, 2)
    partner = me + 1 - 2 * core
    rows = atm_ref.shape[0]
    tiles = rows // tile
    side = lax.rem(me // 2, 2)
    across = lax.rem(me + 2 - 4 * side + devices, devices)
    far = 4 - 4 * core
    direct, passed, joined, plain = 3 - 2 * side, 1 + 2 * side, 4 - 4 * side, 4 * side

    def at(offset):
        return lax.rem(me + offset + devices, devices)

    def copy_to(src, dst, ssem, rsem, device):
        return pltpu.make_async_remote_copy(
            src_ref=src, dst_ref=dst, send_sem=ssem, recv_sem=rsem,
            device_id={"tile": device}, device_id_type=pl.DeviceIdType.MESH,
        )

    loads = [
        pltpu.make_async_copy(part.at[2 * m], even.at[m], local_sem.at[m]) for m in range(5)
    ]
    for c in loads:
        c.start()

    barrier = pltpu.get_barrier_semaphore()
    for o in (1, -1, 2, -2, 4, -4):
        pl.semaphore_signal(
            barrier, inc=1, device_id={"tile": at(o)}, device_id_type=pl.DeviceIdType.MESH
        )
    pl.semaphore_wait(barrier, 6)

    def swap(j):
        return copy_to(part.at[2 * j + 1], odd.at[j], osend.at[j], orecv.at[j], partner)

    def ship(m):
        return copy_to(even.at[m], recv.at[m], psend.at[m], precv.at[m], at(2 * m - 4))

    for j in (passed - core, 3 * core, direct - core, 2 - core):
        swap(j).start()
    for c in loads:
        c.wait()

    def combine(m):
        j = m - 1 + core
        swap(j).wait_recv()

        def body(i, carry):
            at_rows = pl.ds(pl.multiple_of(i * tile, tile), tile)
            total = even[m, at_rows, :].astype(jnp.float32)
            total = total + odd[j, at_rows, :].astype(jnp.float32)
            even[m, at_rows, :] = total.astype(jnp.bfloat16)
            return carry

        lax.fori_loop(0, tiles, body, 0, unroll=2)

    add_on = copy_to(even.at[passed], relayed, rsem.at[0], rsem.at[1], across)
    combine(passed)
    add_on.start()
    combine(far)
    ship(plain).start()
    combine(direct)
    ship(direct).start()
    swap(1 + core).wait_recv()

    def adjoint_mix(i, carry):
        at_rows = pl.ds(pl.multiple_of(i * tile, tile), tile)
        gt[at_rows, :] = lax.dot_general(
            cot_ref[at_rows, :], mix_ref[...], (((1,), (1,)), ((), ())),
            preferred_element_type=jnp.float32,
        )
        total = atm_ref[at_rows, :].astype(jnp.float32)
        total = total + even[2, at_rows, :].astype(jnp.float32)
        total = total + odd[1 + core, at_rows, :].astype(jnp.float32)
        fpad[pl.ds(pl.multiple_of(i * tile + HALO, HALO), tile), :] = total
        return carry

    lax.fori_loop(0, tiles, adjoint_mix, 0, unroll=2)

    def add_parts(slots):
        def body(i, carry):
            at_rows = pl.ds(pl.multiple_of(i * tile, tile), tile)
            pad_rows = pl.ds(pl.multiple_of(i * tile + HALO, HALO), tile)
            total = fpad[pad_rows, :]
            for slot in slots:
                total = total + recv[slot, at_rows, :].astype(jnp.float32)
            fpad[pad_rows, :] = total
            return carry

        lax.fori_loop(0, tiles, body, 0, unroll=2)

    add_on.wait_recv()

    def join(i, carry):
        at_rows = pl.ds(pl.multiple_of(i * tile, tile), tile)
        total = even[joined, at_rows, :].astype(jnp.float32)
        total = total + relayed[at_rows, :].astype(jnp.float32)
        even[joined, at_rows, :] = total.astype(jnp.bfloat16)
        return carry

    lax.fori_loop(0, tiles, join, 0, unroll=2)
    ship(joined).start()
    ship(plain).wait_recv()
    add_parts([plain])
    ship(passed).wait_recv()
    add_parts([passed])
    ship(joined).wait_recv()
    add_parts([joined])

    def edges(pad, low, high, k):
        up = copy_to(pad.at[pl.ds(rows, HALO), :], low, hsend.at[k], hrecv.at[k], at(1))
        down = copy_to(pad.at[pl.ds(HALO, HALO), :], high, hsend.at[k + 1], hrecv.at[k + 1], at(-1))
        return up, down

    def window(pad, i):
        w = pad[pl.ds(pl.multiple_of(i * tile, tile), tile + 2 * HALO), :]
        return w[HALO - 1 : HALO - 1 + tile], w[HALO : HALO + tile], w[HALO + 1 : HALO + 1 + tile]

    fwd_edges = edges(fpad, lo, hi, 0)
    for c in fwd_edges:
        c.start()

    def primal(i, carry):
        at_rows = pl.ds(pl.multiple_of(i * tile, tile), tile)
        before, x, after = window(fpad, i)
        kappa = kappa_ref[at_rows, :]
        th = jnp.tanh(x + kappa * (before + after - 2.0 * x))
        hval_ref[at_rows, :] = th.astype(jnp.bfloat16)
        g = gt[at_rows, :] * (1.0 - th * th)
        gs[at_rows, :] = g
        wpad[pl.ds(pl.multiple_of(i * tile + HALO, HALO), tile), :] = kappa * g
        return carry

    lax.fori_loop(1, tiles - 1, primal, 0)
    for c in fwd_edges:
        c.wait()
    fpad[0:HALO, :] = lo[...]
    fpad[rows + HALO : rows + 2 * HALO, :] = hi[...]
    lax.fori_loop(0, 2, lambda j, c: primal(j * (tiles - 1), c), 0)

    adj_edges = edges(wpad, lo2, hi2, 2)
    for c in adj_edges:
        c.start()

    def adjoint(i, carry):
        at_rows = pl.ds(pl.multiple_of(i * tile, tile), tile)
        before, x, after = window(wpad, i)
        grad = gs[at_rows, :] + before + after - 2.0 * x
        grad_ref[at_rows, :] = grad.astype(jnp.bfloat16)
        own[at_rows, :] = grad.T.astype(jnp.bfloat16)
        return carry

    half = tiles // 2 * tile
    pieces = [(tile, half - tile), (half, rows - tile - half), (0, tile), (rows - tile, tile)]

    def grads(p, m):
        cut = pl.ds(pieces[p][0], pieces[p][1])
        return copy_to(
            own.at[cut, :], near.at[2 * m, cut, :], gsend.at[p, m], grecv.at[p, m], at(4 - 2 * m)
        )

    def hand(p, m, src):
        cut = pl.ds(pieces[p][0], pieces[p][1])
        j = m - 1 + core
        return copy_to(
            src, near.at[2 * j + 1, cut, :], xsend.at[p, j], xrecv.at[p, j], partner
        )

    def relay(p):
        cut = pl.ds(pieces[p][0], pieces[p][1])
        return copy_to(
            near_cut(p, joined), near.at[2 * direct, cut, :],
            gsend.at[p, direct], grecv.at[p, direct], across,
        )

    def own_cut(p):
        return own.at[pl.ds(pieces[p][0], pieces[p][1]), :]

    def near_cut(p, m):
        return near.at[2 * m, pl.ds(pieces[p][0], pieces[p][1]), :]

    lax.fori_loop(1, tiles - 1, adjoint, 0)
    for p in (0, 1):
        grads(p, joined).start()
        grads(p, passed).start()
        hand(p, 2, own_cut(p)).start()
    for c in adj_edges:
        c.wait()
    wpad[0:HALO, :] = lo2[...]
    wpad[rows + HALO : rows + 2 * HALO, :] = hi2[...]
    lax.fori_loop(0, 2, lambda j, c: adjoint(j * (tiles - 1), c), 0)
    for p in (2, 3):
        grads(p, joined).start()
        grads(p, passed).start()
        hand(p, 2, own_cut(p)).start()
    keep = pltpu.make_async_copy(own, near.at[2 * 2], local_sem.at[5])
    keep.start()
    for p in range(4):
        grads(p, joined).wait_recv()
        relay(p).start()
        grads(p, joined).wait_send()
        grads(p, plain).start()
    for p in range(4):
        grads(p, direct).wait_recv()
        hand(p, direct, near_cut(p, direct)).start()
    for p in range(4):
        grads(p, plain).wait_recv()
        hand(p, far, near_cut(p, far)).start()
    for p in range(4):
        grads(p, passed).wait_recv()
        hand(p, passed, near_cut(p, passed)).start()
    keep.wait()
    for p in range(4):
        for j in range(4):
            out = hand(p, j + 1 - core, own_cut(p))
            out.wait_send()
            out.wait_recv()
        grads(p, passed).wait_send()
        grads(p, plain).wait_send()
        relay(p).wait_send()
    for j in range(4):
        swap(j).wait_send()
    for m in (plain, direct, joined):
        ship(m).wait_send()
    add_on.wait_send()


def adjoint_kernel(
    src_ref, slot_ref, near_hbm, mask_ref, mix_ref, w_hbm, hval_ref, grad_ref,
    next_ref, grad_out_ref, ocean_ref, acc, near, wbuf, sems, nsem,
):
    tiles_in = pltpu.make_async_copy(near_hbm, near, nsem.at[0])
    tiles_in.start()
    fetch, per = fetch_all(w_hbm, wbuf, sems)
    clear_all(acc)
    tile = w_hbm.shape[1]

    def mixed(i, carry):
        at_rows = pl.ds(pl.multiple_of(i * tile, tile), tile)
        next_ref[at_rows, :] = jnp.dot(
            hval_ref[at_rows, :], mix_ref[...], preferred_element_type=jnp.float32
        ).astype(jnp.bfloat16)
        grad_out_ref[at_rows, :] = grad_ref[at_rows, :]
        return carry

    lax.fori_loop(0, hval_ref.shape[0] // tile, mixed, 0, unroll=4)
    tiles_in.wait()

    def block(c, carry):
        fetch(c).wait()
        for k in range(per):
            e = c * per + k
            product = jnp.dot(near[slot_ref[e]], wbuf[e], preferred_element_type=jnp.float32)
            acc[src_ref[e]] += product
        return carry

    lax.fori_loop(0, CHUNKS, block, 0)

    def finish(i, carry):
        total = jnp.where(mask_ref[pl.ds(i, 1), :] == 1, acc[i], 0.0)
        ocean_ref[i] = total.T.astype(jnp.bfloat16)
        return carry

    lax.fori_loop(0, acc.shape[0], finish, 0, unroll=4)


def shards(
    ocean_field, ocean_mask, remap_weight, source_tile, target_tile, dest_device,
    atm_state, kappa, mix, cotangent,
):
    devices = lax.axis_size("tile")
    me = lax.axis_index("tile")
    entries, tile, _ = remap_weight.shape
    channels = ocean_field.shape[1]
    ocn = ocean_field.shape[0] // tile
    rows = atm_state.shape[0]
    atm = rows // tile
    slots = SPAN * atm
    dest = lax.dynamic_slice_in_dim(dest_device.reshape(-1), me * entries, entries)
    target = lax.dynamic_slice_in_dim(target_tile, me * entries, entries)
    slot = lax.rem(dest - me + WIN + devices, devices) * atm + target
    mask = ocean_mask.reshape(ocn, tile)
    params = functools.partial(pltpu.CompilerParams, vmem_limit_bytes=VMEM_BYTES)

    vmem = pl.BlockSpec(memory_space=pltpu.VMEM)
    hbm = pl.BlockSpec(memory_space=pl.ANY)
    smem = pl.BlockSpec(memory_space=pltpu.SMEM)
    part = pl.pallas_call(
        forward_kernel,
        out_shape=jax.ShapeDtypeStruct((slots, tile, channels), jnp.bfloat16),
        in_specs=[smem, smem, vmem, vmem, hbm],
        out_specs=hbm,
        scratch_shapes=[
            pltpu.VMEM((slots, tile, channels), jnp.float32),
            pltpu.VMEM((ocn, tile, channels), jnp.bfloat16),
            pltpu.VMEM((entries, tile, tile), jnp.bfloat16),
            pltpu.VMEM((slots, tile, channels), jnp.bfloat16),
            pltpu.SemaphoreType.DMA((CHUNKS,)),
            pltpu.SemaphoreType.DMA((SPAN,)),
        ],
        compiler_params=params(),
        name="remap_forward",
    )(source_tile, slot, ocean_field.reshape(ocn, tile, channels), mask, remap_weight)

    f32 = lambda *shape: pltpu.VMEM(shape, jnp.float32)
    near, grad, hval = pl.pallas_call(
        functools.partial(middle_kernel, devices, tile),
        out_shape=(
            jax.ShapeDtypeStruct((SPAN, rows, channels), jnp.bfloat16),
            jax.ShapeDtypeStruct((rows, channels), jnp.bfloat16),
            jax.ShapeDtypeStruct((rows, channels), jnp.bfloat16),
        ),
        in_specs=[hbm, vmem, vmem, vmem, vmem],
        out_specs=(hbm, vmem, vmem),
        scratch_shapes=[
            pltpu.VMEM((5, rows, channels), jnp.bfloat16),
            pltpu.VMEM((4, rows, channels), jnp.bfloat16),
            pltpu.VMEM((5, rows, channels), jnp.bfloat16),
            pltpu.VMEM((rows, channels), jnp.bfloat16),
            f32(rows + 2 * HALO, channels),
            f32(rows + 2 * HALO, channels),
            f32(rows, channels),
            f32(rows, channels),
            f32(HALO, channels),
            f32(HALO, channels),
            f32(HALO, channels),
            f32(HALO, channels),
            pltpu.VMEM((rows, channels), jnp.bfloat16),
            pltpu.SemaphoreType.DMA((6,)),
            pltpu.SemaphoreType.DMA((4,)),
            pltpu.SemaphoreType.DMA((4,)),
            pltpu.SemaphoreType.DMA((5,)),
            pltpu.SemaphoreType.DMA((5,)),
            pltpu.SemaphoreType.DMA((4,)),
            pltpu.SemaphoreType.DMA((4,)),
            pltpu.SemaphoreType.DMA((4, 5)),
            pltpu.SemaphoreType.DMA((4, 5)),
            pltpu.SemaphoreType.DMA((4, 4)),
            pltpu.SemaphoreType.DMA((4, 4)),
            pltpu.SemaphoreType.DMA((2,)),
        ],
        compiler_params=params(collective_id=0, has_side_effects=True),
        name="exchange_and_step",
    )(part.reshape(SPAN, rows, channels), atm_state, kappa, mix, cotangent)

    atm_next, atm_grad, ocean_grad = pl.pallas_call(
        adjoint_kernel,
        out_shape=(
            jax.ShapeDtypeStruct((rows, channels), jnp.bfloat16),
            jax.ShapeDtypeStruct((rows, channels), jnp.bfloat16),
            jax.ShapeDtypeStruct((ocn, tile, channels), jnp.bfloat16),
        ),
        in_specs=[smem, smem, hbm, vmem, vmem, hbm, vmem, vmem],
        out_specs=(vmem, vmem, vmem),
        scratch_shapes=[
            pltpu.VMEM((ocn, channels, tile), jnp.float32),
            pltpu.VMEM((slots, tile, channels), jnp.bfloat16),
            pltpu.VMEM((entries, tile, tile), jnp.bfloat16),
            pltpu.SemaphoreType.DMA((CHUNKS,)),
            pltpu.SemaphoreType.DMA((1,)),
        ],
        compiler_params=params(),
        name="remap_adjoint",
    )(
        source_tile, slot, near.reshape(slots, tile, channels), mask, mix, remap_weight,
        hval, grad,
    )
    return atm_next, atm_grad, ocean_grad.reshape(ocn * tile, channels)


def solution(mesh):
    both = P(("ens", "tile"), None)
    return jax.shard_map(
        shards,
        mesh=mesh,
        in_specs=(
            both, P("tile"), P("tile", None, None), P("tile"), P(), P(),
            both, P("tile", None), P(), both,
        ),
        out_specs=(both, both, both),
        check_vma=False,
    )
```

```python
import functools

import jax
import jax.numpy as jnp
from jax import lax
from jax.experimental import pallas as pl
from jax.experimental.pallas import tpu as pltpu
from jax.sharding import PartitionSpec as P

WIN = 4
SPAN = 2 * WIN + 1
HALO = 8
CHUNKS = 4
VMEM_BYTES = 56 * 1024 * 1024


def diagonal(row, size):
    eye = lax.broadcasted_iota(jnp.int32, (size, size), 0) == lax.broadcasted_iota(
        jnp.int32, (size, size), 1
    )
    return jnp.where(eye, jnp.broadcast_to(row, (size, size)), 0).astype(jnp.bfloat16)


def fetch_all(w_hbm, wbuf, sems):
    per = w_hbm.shape[0] // CHUNKS

    def fetch(c):
        cut = pl.ds(c * per, per)
        return pltpu.make_async_copy(w_hbm.at[cut], wbuf.at[cut], sems.at[c])

    for c in range(CHUNKS):
        fetch(c).start()
    return fetch, per


def clear_all(acc):
    def clear(i, carry):
        acc[i] = jnp.zeros(acc.shape[1:], acc.dtype)
        return carry

    lax.fori_loop(0, acc.shape[0], clear, 0, unroll=4)


def forward_kernel(src_ref, slot_ref, ocean_ref, mask_ref, w_hbm, out_hbm, acc, xm, wbuf, obuf, sems, osems):
    tile = w_hbm.shape[1]
    fetch, per = fetch_all(w_hbm, wbuf, sems)
    clear_all(acc)

    def mask_tile(i, carry):
        keep = jnp.where(mask_ref[pl.ds(i, 1), :] == 1, 1.0, 0.0)
        xm[i] = jnp.dot(
            diagonal(keep, tile), ocean_ref[i], preferred_element_type=jnp.float32
        ).astype(jnp.bfloat16)
        return carry

    lax.fori_loop(0, xm.shape[0], mask_tile, 0, unroll=8)

    def block(c, carry):
        fetch(c).wait()
        for k in range(per):
            e = c * per + k
            product = jnp.dot(wbuf[e], xm[src_ref[e]], preferred_element_type=jnp.float32)
            acc[slot_ref[e]] += product
        return carry

    lax.fori_loop(0, CHUNKS, block, 0)
    group = acc.shape[0] // SPAN

    def put(o):
        cut = pl.ds(o * group, group)
        return pltpu.make_async_copy(obuf.at[cut], out_hbm.at[cut], osems.at[o])

    def narrow(o, carry):
        for t in range(group):
            obuf[o * group + t] = acc[o * group + t].astype(obuf.dtype)
        put(o).start()
        return carry

    lax.fori_loop(0, SPAN, narrow, 0)
    for o in range(SPAN):
        put(o).wait()


def middle_kernel(
    devices, tile, part, atm_ref, kappa_ref, mix_ref, cot_ref,
    near, grad_ref, hval_ref,
    even, odd, recv, relayed, fpad, wpad, gs, gt, lo, hi, lo2, hi2, own,
    local_sem, osend, orecv, psend, precv, hsend, hrecv, gsend, grecv, xsend, xrecv, rsem,
):
    me = lax.axis_index("tile")
    core = lax.rem(me, 2)
    partner = me + 1 - 2 * core
    rows = atm_ref.shape[0]
    tiles = rows // tile
    side = lax.rem(me // 2, 2)
    across = lax.rem(me + 2 - 4 * side + devices, devices)
    far = 4 - 4 * core
    direct, passed, joined, plain = 3 - 2 * side, 1 + 2 * side, 4 - 4 * side, 4 * side

    def at(offset):
        return lax.rem(me + offset + devices, devices)

    def copy_to(src, dst, ssem, rsem, device):
        return pltpu.make_async_remote_copy(
            src_ref=src, dst_ref=dst, send_sem=ssem, recv_sem=rsem,
            device_id={"tile": device}, device_id_type=pl.DeviceIdType.MESH,
        )

    loads = [
        pltpu.make_async_copy(part.at[2 * m], even.at[m], local_sem.at[m]) for m in range(5)
    ]
    for c in loads:
        c.start()

    barrier = pltpu.get_barrier_semaphore()
    for o in (1, -1, 2, -2, 4, -4):
        pl.semaphore_signal(
            barrier, inc=1, device_id={"tile": at(o)}, device_id_type=pl.DeviceIdType.MESH
        )
    pl.semaphore_wait(barrier, 6)

    def swap(j):
        return copy_to(part.at[2 * j + 1], odd.at[j], osend.at[j], orecv.at[j], partner)

    def ship(m):
        return copy_to(even.at[m], recv.at[m], psend.at[m], precv.at[m], at(2 * m - 4))

    for j in (passed - core, 3 * core, direct - core, 2 - core):
        swap(j).start()
    for c in loads:
        c.wait()

    def combine(m):
        j = m - 1 + core
        swap(j).wait_recv()

        def body(i, carry):
            at_rows = pl.ds(pl.multiple_of(i * tile, tile), tile)
            total = even[m, at_rows, :].astype(jnp.float32)
            total = total + odd[j, at_rows, :].astype(jnp.float32)
            even[m, at_rows, :] = total.astype(jnp.bfloat16)
            return carry

        lax.fori_loop(0, tiles, body, 0, unroll=2)

    add_on = copy_to(even.at[passed], relayed, rsem.at[0], rsem.at[1], across)
    combine(passed)
    add_on.start()
    combine(far)
    ship(plain).start()
    combine(direct)
    swap(1 + core).wait_recv()

    def adjoint_mix(i, carry):
        at_rows = pl.ds(pl.multiple_of(i * tile, tile), tile)
        gt[at_rows, :] = lax.dot_general(
            cot_ref[at_rows, :], mix_ref[...], (((1,), (1,)), ((), ())),
            preferred_element_type=jnp.float32,
        )
        total = atm_ref[at_rows, :].astype(jnp.float32)
        total = total + even[2, at_rows, :].astype(jnp.float32)
        total = total + odd[1 + core, at_rows, :].astype(jnp.float32)
        fpad[pl.ds(pl.multiple_of(i * tile + HALO, HALO), tile), :] = total
        return carry

    lax.fori_loop(0, tiles, adjoint_mix, 0, unroll=2)

    def add_parts(slots):
        def body(i, carry):
            at_rows = pl.ds(pl.multiple_of(i * tile, tile), tile)
            pad_rows = pl.ds(pl.multiple_of(i * tile + HALO, HALO), tile)
            total = fpad[pad_rows, :]
            for slot in slots:
                total = total + recv[slot, at_rows, :].astype(jnp.float32)
            fpad[pad_rows, :] = total
            return carry

        lax.fori_loop(0, tiles, body, 0, unroll=2)

    add_on.wait_recv()
    ship(direct).start()

    def join(i, carry):
        at_rows = pl.ds(pl.multiple_of(i * tile, tile), tile)
        total = even[joined, at_rows, :].astype(jnp.float32)
        total = total + relayed[at_rows, :].astype(jnp.float32)
        even[joined, at_rows, :] = total.astype(jnp.bfloat16)
        return carry

    lax.fori_loop(0, tiles, join, 0, unroll=2)
    ship(joined).start()
    ship(plain).wait_recv()
    add_parts([plain])
    ship(passed).wait_recv()
    add_parts([passed])
    ship(joined).wait_recv()
    add_parts([joined])

    def edges(pad, low, high, k):
        up = copy_to(pad.at[pl.ds(rows, HALO), :], low, hsend.at[k], hrecv.at[k], at(1))
        down = copy_to(pad.at[pl.ds(HALO, HALO), :], high, hsend.at[k + 1], hrecv.at[k + 1], at(-1))
        return up, down

    def window(pad, i):
        w = pad[pl.ds(pl.multiple_of(i * tile, tile), tile + 2 * HALO), :]
        return w[HALO - 1 : HALO - 1 + tile], w[HALO : HALO + tile], w[HALO + 1 : HALO + 1 + tile]

    fwd_edges = edges(fpad, lo, hi, 0)
    for c in fwd_edges:
        c.start()

    def primal(i, carry):
        at_rows = pl.ds(pl.multiple_of(i * tile, tile), tile)
        before, x, after = window(fpad, i)
        kappa = kappa_ref[at_rows, :]
        th = jnp.tanh(x + kappa * (before + after - 2.0 * x))
        hval_ref[at_rows, :] = th.astype(jnp.bfloat16)
        g = gt[at_rows, :] * (1.0 - th * th)
        gs[at_rows, :] = g
        wpad[pl.ds(pl.multiple_of(i * tile + HALO, HALO), tile), :] = kappa * g
        return carry

    lax.fori_loop(1, tiles - 1, primal, 0)
    for c in fwd_edges:
        c.wait()
    fpad[0:HALO, :] = lo[...]
    fpad[rows + HALO : rows + 2 * HALO, :] = hi[...]
    lax.fori_loop(0, 2, lambda j, c: primal(j * (tiles - 1), c), 0)

    adj_edges = edges(wpad, lo2, hi2, 2)
    for c in adj_edges:
        c.start()

    def adjoint(i, carry):
        at_rows = pl.ds(pl.multiple_of(i * tile, tile), tile)
        before, x, after = window(wpad, i)
        grad = gs[at_rows, :] + before + after - 2.0 * x
        grad_ref[at_rows, :] = grad.astype(jnp.bfloat16)
        own[at_rows, :] = grad.T.astype(jnp.bfloat16)
        return carry

    half = tiles // 2 * tile
    pieces = [(tile, half - tile), (half, rows - tile - half), (0, tile), (rows - tile, tile)]

    def grads(p, m):
        cut = pl.ds(pieces[p][0], pieces[p][1])
        return copy_to(
            own.at[cut, :], near.at[2 * m, cut, :], gsend.at[p, m], grecv.at[p, m], at(4 - 2 * m)
        )

    def hand(p, m, src):
        cut = pl.ds(pieces[p][0], pieces[p][1])
        j = m - 1 + core
        return copy_to(
            src, near.at[2 * j + 1, cut, :], xsend.at[p, j], xrecv.at[p, j], partner
        )

    def relay(p):
        cut = pl.ds(pieces[p][0], pieces[p][1])
        return copy_to(
            near_cut(p, joined), near.at[2 * direct, cut, :],
            gsend.at[p, direct], grecv.at[p, direct], across,
        )

    def own_cut(p):
        return own.at[pl.ds(pieces[p][0], pieces[p][1]), :]

    def near_cut(p, m):
        return near.at[2 * m, pl.ds(pieces[p][0], pieces[p][1]), :]

    lax.fori_loop(1, tiles - 1, adjoint, 0)
    for p in (0, 1):
        grads(p, joined).start()
        grads(p, passed).start()
        hand(p, 2, own_cut(p)).start()
    for c in adj_edges:
        c.wait()
    wpad[0:HALO, :] = lo2[...]
    wpad[rows + HALO : rows + 2 * HALO, :] = hi2[...]
    lax.fori_loop(0, 2, lambda j, c: adjoint(j * (tiles - 1), c), 0)
    for p in (2, 3):
        grads(p, joined).start()
        grads(p, passed).start()
        hand(p, 2, own_cut(p)).start()
    keep = pltpu.make_async_copy(own, near.at[2 * 2], local_sem.at[5])
    keep.start()
    for p in range(4):
        grads(p, joined).wait_recv()
        relay(p).start()
        grads(p, joined).wait_send()
        grads(p, plain).start()
    for p in range(4):
        grads(p, direct).wait_recv()
        hand(p, direct, near_cut(p, direct)).start()
    for p in range(4):
        grads(p, plain).wait_recv()
        hand(p, far, near_cut(p, far)).start()
    for p in range(4):
        grads(p, passed).wait_recv()
        hand(p, passed, near_cut(p, passed)).start()
    keep.wait()
    for p in range(4):
        for j in range(4):
            out = hand(p, j + 1 - core, own_cut(p))
            out.wait_send()
            out.wait_recv()
        grads(p, passed).wait_send()
        grads(p, plain).wait_send()
        relay(p).wait_send()
    for j in range(4):
        swap(j).wait_send()
    for m in (plain, direct, joined):
        ship(m).wait_send()
    add_on.wait_send()


def adjoint_kernel(
    src_ref, slot_ref, near_hbm, mask_ref, mix_ref, w_hbm, hval_ref, grad_ref,
    next_ref, grad_out_ref, ocean_ref, acc, near, wbuf, sems, nsem,
):
    tiles_in = pltpu.make_async_copy(near_hbm, near, nsem.at[0])
    tiles_in.start()
    fetch, per = fetch_all(w_hbm, wbuf, sems)
    clear_all(acc)
    tile = w_hbm.shape[1]

    def mixed(i, carry):
        at_rows = pl.ds(pl.multiple_of(i * tile, tile), tile)
        next_ref[at_rows, :] = jnp.dot(
            hval_ref[at_rows, :], mix_ref[...], preferred_element_type=jnp.float32
        ).astype(jnp.bfloat16)
        grad_out_ref[at_rows, :] = grad_ref[at_rows, :]
        return carry

    lax.fori_loop(0, hval_ref.shape[0] // tile, mixed, 0, unroll=4)
    tiles_in.wait()

    def block(c, carry):
        fetch(c).wait()
        for k in range(per):
            e = c * per + k
            product = jnp.dot(near[slot_ref[e]], wbuf[e], preferred_element_type=jnp.float32)
            acc[src_ref[e]] += product
        return carry

    lax.fori_loop(0, CHUNKS, block, 0)

    def finish(i, carry):
        total = jnp.where(mask_ref[pl.ds(i, 1), :] == 1, acc[i], 0.0)
        ocean_ref[i] = total.T.astype(jnp.bfloat16)
        return carry

    lax.fori_loop(0, acc.shape[0], finish, 0, unroll=4)


def shards(
    ocean_field, ocean_mask, remap_weight, source_tile, target_tile, dest_device,
    atm_state, kappa, mix, cotangent,
):
    devices = lax.axis_size("tile")
    me = lax.axis_index("tile")
    entries, tile, _ = remap_weight.shape
    channels = ocean_field.shape[1]
    ocn = ocean_field.shape[0] // tile
    rows = atm_state.shape[0]
    atm = rows // tile
    slots = SPAN * atm
    dest = lax.dynamic_slice_in_dim(dest_device.reshape(-1), me * entries, entries)
    target = lax.dynamic_slice_in_dim(target_tile, me * entries, entries)
    slot = lax.rem(dest - me + WIN + devices, devices) * atm + target
    mask = ocean_mask.reshape(ocn, tile)
    params = functools.partial(pltpu.CompilerParams, vmem_limit_bytes=VMEM_BYTES)

    vmem = pl.BlockSpec(memory_space=pltpu.VMEM)
    hbm = pl.BlockSpec(memory_space=pl.ANY)
    smem = pl.BlockSpec(memory_space=pltpu.SMEM)
    part = pl.pallas_call(
        forward_kernel,
        out_shape=jax.ShapeDtypeStruct((slots, tile, channels), jnp.bfloat16),
        in_specs=[smem, smem, vmem, vmem, hbm],
        out_specs=hbm,
        scratch_shapes=[
            pltpu.VMEM((slots, tile, channels), jnp.float32),
            pltpu.VMEM((ocn, tile, channels), jnp.bfloat16),
            pltpu.VMEM((entries, tile, tile), jnp.bfloat16),
            pltpu.VMEM((slots, tile, channels), jnp.bfloat16),
            pltpu.SemaphoreType.DMA((CHUNKS,)),
            pltpu.SemaphoreType.DMA((SPAN,)),
        ],
        compiler_params=params(),
        name="remap_forward",
    )(source_tile, slot, ocean_field.reshape(ocn, tile, channels), mask, remap_weight)

    f32 = lambda *shape: pltpu.VMEM(shape, jnp.float32)
    near, grad, hval = pl.pallas_call(
        functools.partial(middle_kernel, devices, tile),
        out_shape=(
            jax.ShapeDtypeStruct((SPAN, rows, channels), jnp.bfloat16),
            jax.ShapeDtypeStruct((rows, channels), jnp.bfloat16),
            jax.ShapeDtypeStruct((rows, channels), jnp.bfloat16),
        ),
        in_specs=[hbm, vmem, vmem, vmem, vmem],
        out_specs=(hbm, vmem, vmem),
        scratch_shapes=[
            pltpu.VMEM((5, rows, channels), jnp.bfloat16),
            pltpu.VMEM((4, rows, channels), jnp.bfloat16),
            pltpu.VMEM((5, rows, channels), jnp.bfloat16),
            pltpu.VMEM((rows, channels), jnp.bfloat16),
            f32(rows + 2 * HALO, channels),
            f32(rows + 2 * HALO, channels),
            f32(rows, channels),
            f32(rows, channels),
            f32(HALO, channels),
            f32(HALO, channels),
            f32(HALO, channels),
            f32(HALO, channels),
            pltpu.VMEM((rows, channels), jnp.bfloat16),
            pltpu.SemaphoreType.DMA((6,)),
            pltpu.SemaphoreType.DMA((4,)),
            pltpu.SemaphoreType.DMA((4,)),
            pltpu.SemaphoreType.DMA((5,)),
            pltpu.SemaphoreType.DMA((5,)),
            pltpu.SemaphoreType.DMA((4,)),
            pltpu.SemaphoreType.DMA((4,)),
            pltpu.SemaphoreType.DMA((4, 5)),
            pltpu.SemaphoreType.DMA((4, 5)),
            pltpu.SemaphoreType.DMA((4, 4)),
            pltpu.SemaphoreType.DMA((4, 4)),
            pltpu.SemaphoreType.DMA((2,)),
        ],
        compiler_params=params(collective_id=0, has_side_effects=True),
        name="exchange_and_step",
    )(part.reshape(SPAN, rows, channels), atm_state, kappa, mix, cotangent)

    atm_next, atm_grad, ocean_grad = pl.pallas_call(
        adjoint_kernel,
        out_shape=(
            jax.ShapeDtypeStruct((rows, channels), jnp.bfloat16),
            jax.ShapeDtypeStruct((rows, channels), jnp.bfloat16),
            jax.ShapeDtypeStruct((ocn, tile, channels), jnp.bfloat16),
        ),
        in_specs=[smem, smem, hbm, vmem, vmem, hbm, vmem, vmem],
        out_specs=(vmem, vmem, vmem),
        scratch_shapes=[
            pltpu.VMEM((ocn, channels, tile), jnp.float32),
            pltpu.VMEM((slots, tile, channels), jnp.bfloat16),
            pltpu.VMEM((entries, tile, tile), jnp.bfloat16),
            pltpu.SemaphoreType.DMA((CHUNKS,)),
            pltpu.SemaphoreType.DMA((1,)),
        ],
        compiler_params=params(),
        name="remap_adjoint",
    )(
        source_tile, slot, near.reshape(slots, tile, channels), mask, mix, remap_weight,
        hval, grad,
    )
    return atm_next, atm_grad, ocean_grad.reshape(ocn * tile, channels)


def solution(mesh):
    both = P(("ens", "tile"), None)
    return jax.shard_map(
        shards,
        mesh=mesh,
        in_specs=(
            both, P("tile"), P("tile", None, None), P("tile"), P(), P(),
            both, P("tile", None), P(), both,
        ),
        out_specs=(both, both, both),
        check_vma=False,
    )
```
